256 devices in a mesh: expert: 8 (over y, core), tok: 32 (over z, x).
Axes of the slice: x: 4, y: 4, z: 8, core: 2. Of those that a mesh axis runs over, the one named last changes fastest.
Arguments:
- inputs: bfloat16 [32768, 2048], P(('expert', 'tok')), may hold values from -6 to 6
- cotangent: bfloat16 [32768, 2048], P(('expert', 'tok')), may hold values from -6 to 6
- expert_ids: int32 [32768, 2], P(('expert', 'tok')), may hold values from 0 to 63, all different within a row; in each aligned block of 128 rows (0 to 127, 128 to 255, ...) at most 6 rows name the same one
- gates: bfloat16 [32768, 2], P(('expert', 'tok')), may hold values from 0.099609375 to 1
- w_gate: bfloat16 [8, 2048, 8192], P('expert', None, 'tok'), may hold values from -0.125 to 0.125
- w_up: bfloat16 [8, 2048, 8192], P('expert', None, 'tok'), may hold values from -0.125 to 0.125
- w_down: bfloat16 [8, 8192, 2048], P('expert', 'tok'), may hold values from -0.0625 to 0.0625
Outputs:
- input_grad: bfloat16 [32768, 2048], P(('expert', 'tok'))
- gate_grad: float32 [32768, 2], P(('expert', 'tok'))
- grad_w_gate: float32 [8, 2048, 8192], P('expert', None, 'tok')
- grad_w_up: float32 [8, 2048, 8192], P('expert', None, 'tok')
- grad_w_down: float32 [8, 8192, 2048], P('expert', 'tok')
The draws below stay inside these ranges and needn't reach their ends.
Inputs may be any that keep to these rules, and one draw needn't show every extreme that they name: `expert_ids`: in each aligned block of 128 tokens (the tokens of one device) no expert id occurs more than 6 times, and the two ids of a token differ.
All inputs are finite; a program needn't handle non-finite values.
Results may differ from the reference program's by a relative error of at most 0.0049.
Values may be sent and summed in bfloat16 or wider, within the bound.
No kernel may reach another device: no remote copies, remote signals or barrier semaphores. Data moves between devices by JAX's collectives and lax.ppermute only.
A program may use at most 128 MiB of HBM per device.

```python
import math
import jax
import jax.numpy as jnp
import numpy as np
from jax import lax

D = 2048
FF = 8192
EXPERTS_ALL = 64
TOK_DEV = 128
CAP = 6
EXPERTS = 8
TOKENS = 32768


def block_levels(stream_key, extent, split, low, largest):
    loudness, own = 1.0, jax.random.fold_in(stream_key, 6)
    for axis_at, parts in split:
        steps = jnp.exp(jax.random.uniform(jax.random.fold_in(own, axis_at), (parts,), jnp.float32, low / len(split), largest / len(split)))
        loudness = loudness * jnp.repeat(steps, extent[axis_at] // parts).reshape([-1 if axis == axis_at else 1 for axis in range(len(extent))])
    return loudness


def deal_out(own_key, own, number, rows, amount, top, most, skew):
    ranking = jax.random.permutation(own_key, amount)
    heavy_load, usual = portions_of(amount, rows * top, most, skew, True), portions_of(amount, rows * top, most, skew, False)
    places = jnp.arange(amount)

    def named(sizes, offset_by):
        used = int((sizes > 0).sum())
        fixed = max(1, used // 4)
        moved = fixed + (places - fixed + offset_by * (used - fixed)) % max(1, amount - fixed)
        return jnp.zeros((amount,), jnp.int32).at[ranking[jnp.where(places < fixed, places, moved)]].set(jnp.asarray(sizes, jnp.int32))

    sizes = jnp.where(number % 4 == 0, named(heavy_load, number // 4), named(usual, number - number // 4 - 1))
    mixed = jax.random.permutation(jax.random.fold_in(own, 3), amount)
    giver, sink = mixed[0:amount // 2 * 2:2], mixed[1:amount // 2 * 2:2]
    margin = jnp.minimum(sizes[giver] - 1, most - sizes[sink]) // 2
    margin = jnp.where((giver == ranking[0]) | (sink == ranking[0]) | (sizes[sink] == 0), 0, jnp.maximum(margin, 0))
    moved = jax.random.randint(jax.random.fold_in(own, 4), (amount // 2,), 0, 1 << 20) % (margin + 1)
    sizes = sizes.at[giver].add(-moved).at[sink].add(moved)
    members = jnp.searchsorted(jnp.cumsum(sizes), jnp.arange(rows * top), side="right").astype(jnp.int32)
    table = members.reshape(top, rows).T
    table = table[jax.random.permutation(jax.random.fold_in(own, 1), rows)]
    offset_by = jax.random.randint(jax.random.fold_in(own, 2), (rows, 1), 0, top)
    return jnp.take_along_axis(table, (jnp.arange(top)[None, :] + offset_by) % top, axis=1)


def portions_of(amount, total, reach, skew, full):
    loads = [(1 << 20) // math.isqrt(rank ** skew) + 1 for rank in range(1, amount + 1)]
    largest = reach if full else min(reach, max(-(-total // amount), total * loads[0] // sum(loads)))
    least = 1 if total - largest >= amount - 1 else 0
    holding, surplus = [largest] + [least] * (amount - 1), total - largest - least * (amount - 1)
    while surplus > 0:
        movable = [i for i in range(1, amount) if holding[i] < largest] or [i for i in range(1, amount) if holding[i] < reach]
        whole, left = sum([loads[i] for i in movable]), surplus
        for i in movable:
            addition = min(reach - holding[i], max(1, left * loads[i] // whole), surplus)
            holding[i] = holding[i] + addition
            surplus = surplus - addition
    return np.array(holding)


def centred(key, dims, scale, reach, pieces=(), kind=jnp.bfloat16):
    entries = jax.random.normal(key, dims, jnp.float32) * scale
    if len(pieces) > 0:
        entries = block_levels(key, dims, pieces, -0.22, 0.18) * entries
    return jnp.clip(entries, min=-reach, max=reach).astype(kind)


def setup_inputs(seed: int = 0) -> dict:
    key_of = jax.random.split(jax.random.key(seed), 8)
    inputs = centred(key_of[0], (TOKENS, D), 1.0, 6.0, ((0, 256),))
    cotangent = centred(key_of[1], (TOKENS, D), 1.0, 6.0, ((0, 256),))
    expert_ids_keys = jax.random.split(jax.random.fold_in(key_of[2], 1), TOKENS // TOK_DEV)
    expert_ids_turns = jax.random.permutation(jax.random.fold_in(key_of[2], 3), TOKENS // TOK_DEV)
    expert_ids = jax.vmap(lambda own, number: deal_out(jax.random.fold_in(key_of[2], 2), own, number, TOK_DEV, EXPERTS_ALL, 2, CAP, 2))(expert_ids_keys, expert_ids_turns).reshape((TOKENS, 2))
    gates = jnp.clip(0.099609375 + 0.9003906 * jax.random.uniform(key_of[3], (TOKENS, 2), jnp.float32) ** block_levels(key_of[3], (TOKENS, 2), ((0, 256),), -0.2, 0.2), 0.099609375, 1.0).astype(jnp.bfloat16)
    w_gate = centred(key_of[4], (EXPERTS, D, FF), D ** -0.5, 0.125, ((0, 8), (2, 32)))
    w_up = centred(key_of[5], (EXPERTS, D, FF), D ** -0.5, 0.125, ((0, 8), (2, 32)))
    w_down = centred(key_of[6], (EXPERTS, FF, D), FF ** -0.5, 0.0625, ((0, 8), (1, 32)))
    return dict(inputs=inputs, cotangent=cotangent, expert_ids=expert_ids, gates=gates, w_gate=w_gate, w_up=w_up, w_down=w_down)


def expert_grads(rows_in, cot_rows, gate_rows, wgate, wup, wdown):
    gate_pre = jnp.dot(rows_in, wgate, preferred_element_type=jnp.float32)
    up_pre = jnp.dot(rows_in, wup, preferred_element_type=jnp.float32)
    logistic = jax.nn.sigmoid(gate_pre)
    swished = gate_pre * logistic
    activation = swished * up_pre
    back_proj = jnp.dot(cot_rows, wdown.T, preferred_element_type=jnp.float32)
    scale_col = gate_rows.astype(jnp.float32)[:, None]
    scaled_act = (scale_col * activation).astype(jnp.bfloat16)
    gate_part = jnp.sum(activation * back_proj, axis=1)
    grad_act = scale_col * back_proj
    grad_gate_pre = (grad_act * up_pre * logistic * (1.0 + gate_pre * (1.0 - logistic))).astype(jnp.bfloat16)
    grad_up_pre = (grad_act * swished).astype(jnp.bfloat16)
    grad_down = jnp.dot(scaled_act.T, cot_rows, preferred_element_type=jnp.float32)
    grad_gate = jnp.dot(rows_in.T, grad_gate_pre, preferred_element_type=jnp.float32)
    grad_up = jnp.dot(rows_in.T, grad_up_pre, preferred_element_type=jnp.float32)
    route_terms = jnp.dot(grad_gate_pre, wgate.T, preferred_element_type=jnp.float32)
    route_terms = route_terms + jnp.dot(grad_up_pre, wup.T, preferred_element_type=jnp.float32)
    return route_terms, gate_part, grad_gate, grad_up, grad_down


def reference(inputs, cotangent, expert_ids, gates, w_gate, w_up, w_down):
    blocks = TOKENS // TOK_DEV
    rows_per = blocks * CAP
    flat = expert_ids.reshape(blocks, TOK_DEV * 2).astype(jnp.int32)
    onehot = (flat[:, :, None] == jnp.arange(EXPERTS, dtype=jnp.int32)[None, None, :]).astype(jnp.int32)
    ranks = jnp.cumsum(onehot, axis=1) - onehot
    position = jnp.sum(ranks * onehot, axis=2).astype(jnp.int32)
    block_ids = jnp.arange(blocks, dtype=jnp.int32)[:, None]
    placed = flat * rows_per + block_ids * CAP + position
    dump = EXPERTS * rows_per
    target = jnp.where(flat < EXPERTS, placed, dump).astype(jnp.int32).reshape(-1)
    token_of = jnp.repeat(jnp.arange(TOKENS, dtype=jnp.int32), 2)
    x_buf = jnp.zeros((dump + 1, D), inputs.dtype).at[target].set(inputs[token_of])
    cot_buf = jnp.zeros((dump + 1, D), cotangent.dtype).at[target].set(cotangent[token_of])
    gate_buf = jnp.zeros((dump + 1,), gates.dtype).at[target].set(gates.reshape(-1))
    x_exp = x_buf[:dump].reshape(EXPERTS, rows_per, D)
    cot_exp = cot_buf[:dump].reshape(EXPERTS, rows_per, D)
    gate_exp = gate_buf[:dump].reshape(EXPERTS, rows_per)
    results = lax.map(lambda group: expert_grads(*group), (x_exp, cot_exp, gate_exp, w_gate, w_up, w_down))
    route_terms, gate_part, grad_gate, grad_up, grad_down = results
    route_rows = jnp.concatenate([route_terms.reshape(dump, D), jnp.zeros((1, D), jnp.float32)], axis=0)
    gate_rows = jnp.concatenate([gate_part.reshape(dump), jnp.zeros((1,), jnp.float32)], axis=0)
    pairs = target.reshape(TOKENS, 2)
    input_grad = (route_rows[pairs[:, 0]] + route_rows[pairs[:, 1]]).astype(jnp.bfloat16)
    gate_grad = gate_rows[pairs]
    return input_grad, gate_grad, grad_gate, grad_up, grad_down
```

```python
import jax
import jax.numpy as jnp
from jax import lax
from jax.experimental import pallas as pl
from jax.experimental.pallas import tpu as pltpu
from jax.sharding import PartitionSpec as P

CAP = 6
BF16 = jnp.bfloat16
F32 = jnp.float32
GATE_COLS = 128


def slot_targets(expert_ids, expert_count):
    flat = expert_ids.reshape(-1)
    onehot = (flat[:, None] == jnp.arange(expert_count, dtype=jnp.int32)[None, :]).astype(jnp.int32)
    ranks = jnp.cumsum(onehot, axis=0) - onehot
    position = jnp.sum(ranks * onehot, axis=1)
    target = jnp.where(flat < expert_count, flat * CAP + position, -1)
    return target.reshape(expert_ids.shape)


def contract_rows(left, right):
    return lax.dot_general(left, right, (((0,), (0,)), ((), ())), preferred_element_type=F32)


def contract_cols(left, right):
    return lax.dot_general(left, right, (((1,), (1,)), ((), ())), preferred_element_type=F32)


REGROUP = []
for _y in range(4):
    for _c in range(2):
        for _z in range(8):
            for _x in range(4):
                _own = _c == _x // 2
                _tc, _tx = (_c, _x) if _own else (1 - _c, 3 - _x)
                REGROUP.append(((_y * 2 + _c) * 32 + _z * 4 + _x, (_y * 2 + _tc) * 32 + _z * 4 + _tx))
CORES = [(i, i ^ 1) for i in range(8)]
PAIR = [(i, i ^ 1) for i in range(32)]
UP = [(z * 4 + x, (z + 1) % 8 * 4 + x) for z in range(8) for x in range(4)]
DOWN = [(z * 4 + x, (z + 7) % 8 * 4 + x) for z in range(8) for x in range(4)]


def regroup(a):
    return lax.ppermute(a, ("expert", "tok"), REGROUP)


def cores(a):
    return lax.ppermute(a, "expert", CORES)


def pair(a):
    return lax.ppermute(a, "tok", PAIR)


def up(a):
    return lax.ppermute(a, "tok", UP)


def down(a):
    return lax.ppermute(a, "tok", DOWN)


def together(*values):
    return lax.optimization_barrier(values)


def assemble(x_pieces, c_pieces):
    arrays, plan = [], []
    for which, pieces in enumerate((x_pieces, c_pieces)):
        offset = 0
        for array, first, last in pieces:
            if not any(array is a for a in arrays):
                arrays.append(array)
            index = [array is a for a in arrays].index(True)
            plan.append((index, first, last, which, offset))
            offset += last - first
    shape = (32,) + arrays[0].shape[1:]

    def kernel(*refs):
        ins, outs = refs[:len(arrays)], refs[len(arrays):]
        for index, first, last, which, offset in plan:
            outs[which][offset:offset + last - first] = ins[index][first:last]

    size = 2 * shape[0] * shape[1] * shape[2] * 2
    return pl.pallas_call(
        kernel,
        out_shape=(jax.ShapeDtypeStruct(shape, BF16), jax.ShapeDtypeStruct(shape, BF16)),
        in_specs=[pl.BlockSpec(memory_space=pltpu.VMEM)] * len(arrays),
        out_specs=(pl.BlockSpec(memory_space=pltpu.VMEM),) * 2,
        compiler_params=pltpu.CompilerParams(vmem_limit_bytes=32 * 2**20),
        cost_estimate=pl.CostEstimate(flops=0, bytes_accessed=2 * size, transcendentals=0),
    )(*arrays)


def gather_rows(first, second, weights):
    wgate, wup, wdown = weights
    near, up1, down1 = together(pair(first), up(second[::-1]), down(second))
    xa, ca = jnp.stack([first[0], near[0]]), jnp.stack([first[1], near[1]])
    up2, down2, side2, wgate = together(
        up(jnp.concatenate([up1[:1], ca, up1[1:], xa])),
        down(jnp.concatenate([ca, down1[1:], xa, down1[:1]])),
        pair(jnp.concatenate([down1[:1], up1[1:], second[:1], down1[1:], up1[:1], second[1:]])),
        regroup(wgate),
    )
    up3, down3, side3, wup, wgate2 = together(
        up(up2), down(down2), pair(jnp.stack([down2[5], up2[3], down2[2], up2[0]])), regroup(wup), cores(wgate)
    )
    up4, down4, side4, wdown, wup2 = together(
        up(up3[1:]), down(down3[:5]), pair(jnp.stack([down3[5], up3[3], down3[2], up3[0]])), regroup(wdown), cores(wup)
    )
    up5, down5, side5, wdown2 = together(
        up(up4[3:]), down(down4[:2]), pair(jnp.stack([up4[2], down4[2]])), cores(wdown)
    )
    x_all, c_all = assemble(
        [
            (up5, 0, 2), (side5, 0, 1), (down4, 3, 5), (up4, 2, 5), (side4, 0, 2), (down3, 3, 6), (up3, 3, 6),
            (side3, 0, 2), (down2, 3, 6), (up2, 3, 6), (side2, 0, 3), (down1, 0, 1), (up1, 1, 2),
            (first, 0, 1), (near, 0, 1), (second, 0, 1),
        ],
        [
            (down5, 0, 2), (side5, 1, 2), (down4, 0, 3), (up4, 0, 2), (side4, 2, 4), (down3, 0, 3), (up3, 0, 3),
            (side3, 2, 4), (down2, 0, 3), (up2, 0, 3), (side2, 3, 6), (down1, 1, 2), (up1, 0, 1),
            (first, 1, 2), (near, 1, 2), (second, 1, 2),
        ],
    )
    return x_all, c_all, (wgate, wup, wdown), (wgate2, wup2, wdown2)


STEPS = [(1, 1, 1), (3, 2, 2), (3, 3, 2), (3, 3, 3), (1, 1, 0)]


def scatter_rows(terms, r, totals):
    parts, at = [], 0
    for counts in STEPS:
        row = []
        for n in counts:
            row.append(terms[at:at + n * r])
            at += n * r
        parts.append(row)
    own = terms[at:]

    def send(route, *pieces):
        return route(jnp.concatenate([p.astype(BF16) for p in pieces]))

    def wide(a):
        return a.astype(F32)

    u, d, s = parts[0]
    u1, d1, s1, *sums = together(send(up, u), send(down, d), send(pair, s), *totals())
    u, d, s = parts[1]
    u2, d2, s2 = together(
        send(up, u[:r] + wide(u1), u[r:2 * r], u[2 * r:] + wide(s1)),
        send(down, d[:r], d[r:] + wide(d1)),
        send(pair, s),
    )
    u, d, s = parts[2]
    u3, d3, s3, grad0 = together(
        send(up, u[:2 * r] + wide(u2[:2 * r]), u[2 * r:] + wide(u2[2 * r:]) + wide(s2[:r])),
        send(down, d[:r] + wide(s2[r:]), d[r:] + wide(d2)),
        send(pair, s),
        regroup(sums[0]),
    )
    u, d, s = parts[3]
    u4, d4, s4 = together(
        send(up, u[:2 * r] + wide(u3[:2 * r]), u[2 * r:] + wide(u3[2 * r:]) + wide(s3[:r])),
        send(down, d[:r] + wide(d3[:r]) + wide(s3[r:]), d[r:] + wide(d3[r:])),
        send(pair, s),
    )
    u, d, _ = parts[4]
    both = own[:2 * r] + wide(u4[:2 * r]) + wide(d4[r:])
    u5, d5, s5, grad1 = together(
        send(up, u + wide(u4[2 * r:]) + wide(s4[:r])),
        send(down, d + wide(d4[:r]) + wide(s4[r:2 * r])),
        send(pair, both[r:]),
        regroup(sums[1]),
    )
    done = jnp.concatenate([
        both[:r] + wide(s5),
        own[2 * r:] + wide(u5) + wide(d5) + wide(s4[2 * r:]),
    ]).astype(BF16)
    home, sum2 = together(regroup(done), sums[2])
    return home, (grad0, grad1, regroup(sum2))


def hidden(x, cot, wgate, wup, wdown):
    gate_pre = jnp.dot(x, wgate, preferred_element_type=F32)
    up_pre = jnp.dot(x, wup, preferred_element_type=F32)
    back = contract_cols(cot, wdown)
    logistic = jax.nn.sigmoid(gate_pre)
    swished = gate_pre * logistic
    activation = swished * up_pre
    gate_part = jnp.sum(activation * back, axis=1)
    d_gate = (back * up_pre * logistic * (1.0 + gate_pre * (1.0 - logistic))).astype(BF16)
    d_up = (back * swished).astype(BF16)
    return activation.astype(BF16), d_gate, d_up, gate_part


def body(inputs, cotangent, expert_ids, gates, w_gate, w_up, w_down):
    tokens, width = inputs.shape
    expert_count = lax.axis_size("expert")
    slots = expert_count * CAP
    half = slots // 2

    target = slot_targets(expert_ids, expert_count)
    hits = target[:, :, None] == jnp.arange(slots, dtype=jnp.int32)[None, None, :]
    select = jnp.sum(hits.astype(F32), axis=1).astype(BF16)
    gated = jnp.sum(hits.astype(F32) * gates.astype(F32)[:, :, None], axis=1).astype(BF16)
    x_buf = contract_rows(select, inputs).astype(BF16)
    cot_buf = contract_rows(gated, cotangent).astype(BF16)
    sent = jnp.stack([x_buf.reshape(expert_count, CAP, width), cot_buf.reshape(expert_count, CAP, width)], axis=1)
    recv = lax.all_to_all(sent, "expert", split_axis=0, concat_axis=0, tiled=True)
    local = regroup(recv.transpose(1, 0, 2, 3).reshape(2, slots, width))

    x_all, c_all, mine, other = gather_rows(local[:, :half], local[:, half:], (w_gate[0], w_up[0], w_down[0]))
    x_all, c_all = x_all.reshape(-1, width), c_all.reshape(-1, width)

    def weight_parts(act, dg, du):
        return contract_rows(x_all, dg), contract_rows(x_all, du), contract_rows(act, c_all)

    act_o, dg_o, du_o, gp_o = hidden(x_all, c_all, *other)
    swapped = [cores(p.astype(BF16)) for p in weight_parts(act_o, dg_o, du_o)]
    act_m, dg_m, du_m, gp_m = hidden(x_all, c_all, *mine)
    terms = (
        contract_cols(dg_m, mine[0]) + contract_cols(du_m, mine[1])
        + contract_cols(dg_o, other[0]) + contract_cols(du_o, other[1])
    )
    gate_part = jnp.broadcast_to((gp_m + gp_o)[:, None], (terms.shape[0], GATE_COLS))
    terms, *swapped = together(jnp.concatenate([terms, gate_part], axis=1), *swapped)

    def totals():
        own = weight_parts(act_m, dg_m, du_m)
        return [(a + b.astype(F32)).astype(BF16) for a, b in zip(own, swapped)]

    home, grads = scatter_rows(terms, half, totals)
    grads = [g.astype(F32)[None] for g in grads]

    moved = lax.all_to_all(
        home.reshape(expert_count, CAP, width + GATE_COLS), "expert", split_axis=0, concat_axis=0, tiled=True
    ).reshape(slots, width + GATE_COLS)
    input_grad = jnp.dot(select, moved[:, :width], preferred_element_type=F32).astype(BF16)
    gate_back = moved[:, width].astype(F32)
    gate_grad = jnp.sum(jnp.where(hits, gate_back[None, None, :], 0.0), axis=2) / gates.astype(F32)
    return (input_grad, gate_grad, *grads)


def solution(mesh):
    return jax.shard_map(
        body,
        mesh=mesh,
        in_specs=(
            P(("expert", "tok"), None),
            P(("expert", "tok"), None),
            P(("expert", "tok"), None),
            P(("expert", "tok"), None),
            P("expert", None, "tok"),
            P("expert", None, "tok"),
            P("expert", "tok", None),
        ),
        out_specs=(
            P(("expert", "tok"), None),
            P(("expert", "tok"), None),
            P("expert", None, "tok"),
            P("expert", None, "tok"),
            P("expert", "tok", None),
        ),
        check_vma=False,
    )
```
